128 devices in a mesh: rows: 32 (over z, x, core), cols: 4 (over y).
Axes of the slice: x: 4, y: 4, z: 4, core: 2. Of those that a mesh axis runs over, the one named last changes fastest.
Arguments:
- trial_block: bfloat16 [294912, 512], P('rows', 'cols'), may hold values from -6 to 6
- ham_blocks: bfloat16 [2304, 9, 128, 128], P('rows'), may hold values from -0.1875 to 0.1875
- partner: int32 [2304, 9], P('rows'), may hold values from 0 to 79, as said below
- live_slots: int32 [32], P('rows'), may hold values from 36 to 72, as said below
Outputs:
- filtered: bfloat16 [294912, 512], P('rows', 'cols')
- gram: float32 [512, 512], P('rows', 'cols')
The draws below stay inside these ranges and needn't reach their ends.
Inputs may be any that keep to these rules, and one draw needn't show every extreme that they name: `partner`: each k of a slot s names a different slot of s + 4 - 4 to s + 8, and the first names s + 4 itself. `live_slots`: some owner has 72 live slots and another the least value.
All inputs are finite; a program needn't handle non-finite values.
Results may differ from the reference program's by a relative error of at most 0.007.
Values may be sent and summed in bfloat16 or wider, within the bound.
A program may use at most 128 MiB of HBM per device.

```python
import jax
import jax.numpy as jnp
from jax import lax

NS = 512
B = 128
HW = 4
K = 9
S = 72
OWNERS = 32
TOTAL_ROWS = 294912


def draw_partner(key, part):
    key = jax.random.fold_in(key, 11)
    total_slots = OWNERS * S
    keys = jax.random.split(key, total_slots)
    perms = jax.vmap(lambda one_key: jax.random.permutation(one_key, 2 * HW))(keys)[:, :K - 1]
    offsets = jnp.where(perms < HW, perms - HW, perms - HW + 1)
    local_slot = (jnp.arange(total_slots, dtype=jnp.int32) % S)[:, None]
    others = local_slot + HW + offsets
    return jnp.concatenate([local_slot + HW, others], axis=1).astype(jnp.int32)


def draw_live_slots(key, part):
    key = jax.random.fold_in(key, 23)
    key_counts, key_place = jax.random.split(key)
    least = max(2 * HW, S // 2)
    counts = jax.random.randint(key_counts, (OWNERS,), least, S + 1)
    place = jax.random.randint(key_place, (), 0, OWNERS)
    counts = counts.at[place].set(S)
    counts = counts.at[(place + 1) % OWNERS].set(least)
    return counts.astype(jnp.int32)


def level_of(rng, dims, cuts, low, largest):
    def one(position, blocks):
        draws = jax.random.uniform(jax.random.fold_in(jax.random.fold_in(rng, 6), position), (blocks,), jnp.float32, low / len(cuts), largest / len(cuts))
        return jnp.repeat(jnp.exp(draws), dims[position] // blocks).reshape((-1,) + (1,) * (len(dims) - position - 1))

    level = one(*cuts[0])
    for cut in cuts[1:]:
        level = level * one(*cut)
    return level


def gaussian(rng, dims, deviation, reach, cuts=(), kind=jnp.bfloat16):
    factor_of = level_of(rng, dims, cuts, -0.22, 0.18) if cuts else 1.0
    array = jax.random.normal(rng, dims, jnp.float32) * deviation * factor_of
    return jnp.minimum(jnp.maximum(array, -reach), reach).astype(kind)


def setup_inputs(seed: int = 0) -> dict:
    seeds = jax.random.split(jax.random.key(seed), 5)
    trial_block = gaussian(seeds[0], (TOTAL_ROWS, NS), 1.0, 6.0, ((0, 32), (1, 4)))
    ham_blocks = gaussian(seeds[1], (TOTAL_ROWS // B, K, B, B), (K * B) ** -0.5, 0.1875, ((0, 32),))
    partner = draw_partner(jax.random.fold_in(seeds[4], 71), 0)
    live_slots = draw_live_slots(jax.random.fold_in(seeds[4], 71), 0)
    return dict(trial_block=trial_block, ham_blocks=ham_blocks, partner=partner, live_slots=live_slots)


CENTER = 0.5
HALF_WIDTH = 1.5


def reference(trial_block, ham_blocks, partner, live_slots):
    slot_ids = jnp.arange(S, dtype=jnp.int32)
    keeps = (slot_ids[None, :] < HW) | (slot_ids[None, :] >= HW + S - live_slots[:, None])
    row_keep = jnp.repeat(keeps.reshape(-1), B)[:, None]
    blocks_all = ham_blocks.reshape(OWNERS, S, K, B, B)
    links = partner.reshape(OWNERS, S, K)

    def operator(vectors):
        padded = jnp.pad(vectors.reshape(OWNERS * S, B, NS), ((HW, HW), (0, 0), (0, 0)))

        def one_owner(packed):
            owner, blocks, link = packed
            window = lax.dynamic_slice_in_dim(padded, owner * S, S + 2 * HW, 0)
            picked = window[link].astype(jnp.float32)
            return jnp.einsum("skab,skbc->sac", blocks.astype(jnp.float32), picked)

        result = lax.map(one_owner, (jnp.arange(OWNERS, dtype=jnp.int32), blocks_all, links))
        return result.reshape(OWNERS * S * B, NS)

    start = jnp.where(row_keep, trial_block, jnp.zeros_like(trial_block))
    start_wide = start.astype(jnp.float32)
    first = jnp.where(row_keep, (operator(start) - CENTER * start_wide) / HALF_WIDTH, jnp.float32(0.0)).astype(jnp.bfloat16)
    first_wide = first.astype(jnp.float32)
    second_wide = 2.0 * (operator(first) - CENTER * first_wide) / HALF_WIDTH - start_wide
    filtered = jnp.where(row_keep, second_wide, jnp.float32(0.0)).astype(jnp.bfloat16)
    gram = jnp.dot(filtered.T, filtered, preferred_element_type=jnp.float32) / (OWNERS * S * B)
    return filtered, gram
```

```python
import functools

import jax
import jax.numpy as jnp
from jax import lax
from jax.experimental import pallas as pl
from jax.experimental.pallas import tpu as pltpu
from jax.sharding import PartitionSpec as P

MESH = pl.DeviceIdType.MESH
HW = 4
B = 128
S = 72
K = 9
GS = 4
NG = S // GS
NS = 512
CENTER = 0.5
HALF_WIDTH = 1.5
BF = jnp.bfloat16
F32 = jnp.float32


def kernel(trial, ham, partner, live, filt, gram,
           hbuf, v0, v1, land0, land1, fout, recv, gacc,
           core_out, core_in, acc, a_out, a_in, b_out, b_in,
           a2, b2, a2_out, b2_out, a3_in, b3_in, tile, tile_in,
           h_sem, t_sem, f_sem, halo_s, halo_r, y_s, y_r, c_s, c_r, p_s, p_r, q_s, q_r, w_s, w_r):
    row = lax.axis_index("rows")
    col = lax.axis_index("cols")
    core = lax.rem(row, 2)
    px = lax.rem(row // 2, 4)
    pz = row // 8
    after = (lax.rem(row + 1, 32), col)
    before = (lax.rem(row + 31, 32), col)
    mate = (row + 1 - 2 * core, col)

    def at_y(d):
        return (row, lax.rem(col + d, 4))

    def at_x(d):
        return (pz * 8 + lax.rem(px + d, 4) * 2 + core, col)

    def at_z(d):
        return (lax.rem(pz + d, 4) * 8 + px * 2 + core, col)

    peers = [after, before, mate] + [f(d) for f in (at_x, at_y, at_z) for d in (1, 2, 3)]
    barrier = pltpu.get_barrier_semaphore()
    for peer in peers:
        pl.semaphore_signal(barrier, inc=1, device_id=peer, device_id_type=MESH)

    def remote(src, dst, ssem, rsem, peer):
        return pltpu.make_async_remote_copy(
            src_ref=src, dst_ref=dst, send_sem=ssem, recv_sem=rsem,
            device_id=peer, device_id_type=MESH)

    load_trial = pltpu.make_async_copy(trial, v0.at[pl.ds(HW, S)], t_sem.at[0])
    load_trial.start()

    def load_ham(b):
        part = pl.ds(b * GS, GS)
        return pltpu.make_async_copy(ham.at[part], hbuf.at[part], h_sem.at[b])

    def block_of(i):
        return lax.rem(i + 1, NG)

    lax.fori_loop(0, NG, lambda i, c: (load_ham(block_of(i)).start(), c)[1], 0)
    load_trial.wait()

    count = live[0]

    def keep(s):
        return (s < HW) | (s >= HW + S - count)

    def mask(s, c):
        v0[s + HW] = jnp.where(keep(s), v0[s + HW].astype(F32), 0.0).astype(BF)
        return c

    lax.fori_loop(HW, S - 32, mask, 0)

    def product(src, s):
        lhs = jnp.concatenate([hbuf[s, k] for k in range(K)], axis=1)
        rhs = jnp.concatenate([src[partner[s, k]] for k in range(K)], axis=0)
        return jnp.dot(lhs, rhs, preferred_element_type=F32)

    def first_step(b):
        for j in range(GS):
            s = b * GS + j
            value = (product(v0, s) - CENTER * v0[s + HW].astype(F32)) * (1.0 / HALF_WIDTH)
            v1[s + HW] = jnp.where(keep(s), value, 0.0).astype(BF)

    def second_step(g):
        for j in range(GS):
            s = g * GS + j
            value = (product(v1, s) - CENTER * v1[s + HW].astype(F32)) * (2.0 / HALF_WIDTH)
            value = value - v0[s + HW].astype(F32)
            fout[s] = jnp.where(keep(s), value, 0.0).astype(BF)

    def store_out(g):
        part = pl.ds(g * GS, GS)
        return pltpu.make_async_copy(fout.at[part], filt.at[part], f_sem.at[g])

    def to_col(g, t, d):
        there = lax.rem(col + d, 4)
        return remote(fout.at[g * GS + there], recv.at[t, col], y_s.at[t, d - 1], y_r.at[t, d - 1], at_y(d))

    def from_col(t, d):
        origin = lax.rem(col + 4 - d, 4)
        return remote(fout.at[0], recv.at[t, origin], y_s.at[t, d - 1], y_r.at[t, d - 1], at_y(d))

    def hand_out(g, t):
        for d in (2, 1, 3):
            to_col(g, t, d).start()
        store_out(g).start()
        recv[t, col] = fout[g * GS + col]

    def prologue(i, c):
        b = block_of(i)
        load_ham(b).wait()
        first_step(b)
        return c

    lax.fori_loop(0, 2, prologue, 0)

    pl.semaphore_wait(barrier, len(peers))

    def halo(src, first, land, n):
        return (
            remote(src.at[pl.ds(first + S - HW, HW)], land.at[0], halo_s.at[n], halo_r.at[n], after),
            remote(src.at[pl.ds(first, HW)], land.at[1], halo_s.at[n + 1], halo_r.at[n + 1], before),
        )

    def place(land, dst):
        for j in range(HW):
            dst[j] = jnp.where(row > 0, land[0, j].astype(F32), 0.0).astype(BF)
            dst[j + HW + S] = jnp.where(row < 31, land[1, j].astype(F32), 0.0).astype(BF)

    halo0 = halo(trial, 0, land0, 0)
    for copy in halo0:
        copy.start()

    def main(i, c):
        b = block_of(i)

        @pl.when(i == NG - 2)
        def _():
            for copy in halo0:
                copy.wait()
            place(land0, v0)

        load_ham(b).wait()
        first_step(b)
        g = jnp.where(i == NG - 1, 1, i)
        second_step(g)
        hand_out(g, i - 2)
        return c

    lax.fori_loop(2, NG, main, 0)

    halo1 = halo(v1, HW, land1, 2)
    for copy in halo1:
        copy.start()
    for copy in halo1:
        copy.wait()
    place(land1, v1)

    def ends(n, c):
        g = n * (NG - 1)
        second_step(g)
        hand_out(g, NG - 2 + n)
        return c

    lax.fori_loop(0, 2, ends, 0)

    gacc[...] = jnp.zeros_like(gacc)

    def gram_step(n, c):
        for u in range(2):
            for d in (1, 2, 3):
                from_col(2 * n + u, d).wait_recv()
        rows = [jnp.concatenate([recv[2 * n + u, q] for q in range(4)], axis=1) for u in range(2)]
        x = jnp.concatenate(rows, axis=0)
        part = lax.dot_general(x, x, (((0,), (0,)), ((), ())), preferred_element_type=F32)
        gacc[...] += part.reshape(gacc.shape)
        return c

    lax.fori_loop(0, NG // 2, gram_step, 0)

    for n in range(16):
        core_out[n] = gacc[2 * n + 1 - core].astype(BF)
    to_mate = remote(core_out, core_in, c_s.at[0], c_r.at[0], mate)
    to_mate.start()
    to_mate.wait()

    for n in range(16):
        acc[n] = gacc[2 * n + core] + core_in[n].astype(F32)
    copies = []
    for d in (2, 1, 3):
        there = lax.rem(px + d, 4)
        for z in range(4):
            a_out[d - 1, z] = acc[z * 4 + there, :, 0:256].astype(BF)
        copies.append(remote(a_out.at[d - 1], a_in.at[d - 1], p_s.at[0, d - 1], p_r.at[0, d - 1], at_x(d)))
        copies[-1].start()
        there = lax.rem(pz + d, 4)
        for x in range(4):
            b_out[d - 1, x] = acc[there * 4 + x, :, 256:512].astype(BF)
        copies.append(remote(b_out.at[d - 1], b_in.at[d - 1], p_s.at[1, d - 1], p_r.at[1, d - 1], at_z(d)))
        copies[-1].start()
    for copy in copies:
        copy.wait()
    for n in range(4):
        a2[n] = acc[n * 4 + px, :, 0:256] + sum(a_in[d, n].astype(F32) for d in range(3))
        b2[n] = acc[pz * 4 + n, :, 256:512] + sum(b_in[d, n].astype(F32) for d in range(3))
    copies = []
    for d in (2, 1, 3):
        a2_out[d - 1] = a2[lax.rem(pz + d, 4)].astype(BF)
        copies.append(remote(a2_out.at[d - 1], a3_in.at[d - 1], q_s.at[0, d - 1], q_r.at[0, d - 1], at_z(d)))
        copies[-1].start()
        b2_out[d - 1] = b2[lax.rem(px + d, 4)].astype(BF)
        copies.append(remote(b2_out.at[d - 1], b3_in.at[d - 1], q_s.at[1, d - 1], q_r.at[1, d - 1], at_x(d)))
        copies[-1].start()
    for copy in copies:
        copy.wait()
    a3 = a2[pz] + sum(a3_in[d].astype(F32) for d in range(3))
    b3 = b2[px] + sum(b3_in[d].astype(F32) for d in range(3))
    for q in range(2):
        tile[q] = a3[:, q * 128:(q + 1) * 128]
        tile[q + 2] = b3[:, q * 128:(q + 1) * 128]

    copies = [
        remote(tile.at[lax.rem(col + d, 4)], tile_in.at[d - 1], w_s.at[d - 1], w_r.at[d - 1], at_y(d))
        for d in (2, 1, 3)
    ]
    for copy in copies:
        copy.start()
    for copy in copies:
        copy.wait()
    gram[...] = (tile[col] + (tile_in[0] + tile_in[1] + tile_in[2])) * (1.0 / (32 * S * B))

    def finish(t, c):
        for d in (1, 2, 3):
            from_col(t, d).wait_send()
        store_out(t).wait()
        return c

    lax.fori_loop(0, NG, finish, 0)


def body(trial_block, ham_blocks, partner, live_slots):
    dma = pltpu.SemaphoreType.DMA
    any_space = pl.BlockSpec(memory_space=pl.ANY)
    smem = pl.BlockSpec(memory_space=pltpu.SMEM)
    filtered, gram = pl.pallas_call(
        kernel,
        out_shape=(
            jax.ShapeDtypeStruct((S, B, B), BF),
            jax.ShapeDtypeStruct((16, 128), F32),
        ),
        in_specs=[any_space, any_space, smem, smem],
        out_specs=(any_space, pl.BlockSpec(memory_space=pltpu.VMEM)),
        scratch_shapes=[
            pltpu.VMEM((S, K, B, B), BF),
            pltpu.VMEM((S + 2 * HW, B, B), BF),
            pltpu.VMEM((S + 2 * HW, B, B), BF),
            pltpu.VMEM((2, HW, B, B), BF),
            pltpu.VMEM((2, HW, B, B), BF),
            pltpu.VMEM((S, B, B), BF),
            pltpu.VMEM((NG, 4, B, B), BF),
            pltpu.VMEM((32, 16, NS), F32),
            pltpu.VMEM((16, 16, NS), BF),
            pltpu.VMEM((16, 16, NS), BF),
            pltpu.VMEM((16, 16, NS), F32),
            pltpu.VMEM((3, 4, 16, 256), BF),
            pltpu.VMEM((3, 4, 16, 256), BF),
            pltpu.VMEM((3, 4, 16, 256), BF),
            pltpu.VMEM((3, 4, 16, 256), BF),
            pltpu.VMEM((4, 16, 256), F32),
            pltpu.VMEM((4, 16, 256), F32),
            pltpu.VMEM((3, 16, 256), BF),
            pltpu.VMEM((3, 16, 256), BF),
            pltpu.VMEM((3, 16, 256), BF),
            pltpu.VMEM((3, 16, 256), BF),
            pltpu.VMEM((4, 16, 128), F32),
            pltpu.VMEM((3, 16, 128), F32),
            dma((NG,)),
            dma((1,)),
            dma((NG,)),
            dma((4,)),
            dma((4,)),
            dma((NG, 3)),
            dma((NG, 3)),
            dma((1,)),
            dma((1,)),
            dma((2, 3)),
            dma((2, 3)),
            dma((2, 3)),
            dma((2, 3)),
            dma((3,)),
            dma((3,)),
        ],
        compiler_params=pltpu.CompilerParams(
            collective_id=0, has_side_effects=True, vmem_limit_bytes=50 << 20),
        name="filter_gram",
    )(trial_block.reshape(S, B, B), ham_blocks, partner, live_slots)
    return filtered.reshape(S * B, B), gram


def solution(mesh):
    return jax.shard_map(
        body,
        mesh=mesh,
        in_specs=(P("rows", "cols"), P("rows", None, None, None), P("rows", None), P("rows")),
        out_specs=(P("rows", "cols"), P("rows", "cols")),
        check_vma=False,
    )
```

```python
import functools

import jax
import jax.numpy as jnp
from jax import lax
from jax.experimental import pallas as pl
from jax.experimental.pallas import tpu as pltpu
from jax.sharding import PartitionSpec as P

MESH = pl.DeviceIdType.MESH
HW = 4
B = 128
S = 72
K = 9
GS = 4
NG = S // GS
HEAD = 20
NS = 512
CENTER = 0.5
HALF_WIDTH = 1.5
BF = jnp.bfloat16
F32 = jnp.float32


def kernel(trial, ham, partner_in, live_in, filt, gram,
           partner, live, hbuf, v0a, v0, v1, land0, land1, recv, gacc,
           core_out, core_in, tiles_out, tiles_in, own,
           m_sem, h_sem, t_sem, halo_s, halo_r, y_s, y_r, c_s, c_r, p_s, p_r):
    row = lax.axis_index("rows")
    col = lax.axis_index("cols")
    core = lax.rem(row, 2)
    px = lax.rem(row // 2, 4)
    pz = row // 8
    after = (lax.rem(row + 1, 32), col)
    before = (lax.rem(row + 31, 32), col)
    mate = (row + 1 - 2 * core, col)

    def at_y(d):
        return (row, lax.rem(col + d, 4))

    def at_plane(dz, dx):
        return (lax.rem(pz + dz, 4) * 8 + lax.rem(px + dx, 4) * 2 + core, col)

    peers = [after, before, mate] + [at_y(d) for d in (1, 2, 3)]
    peers += [at_plane(n // 4, n % 4) for n in range(1, 16)]
    barrier = pltpu.get_barrier_semaphore()
    for peer in peers:
        pl.semaphore_signal(barrier, inc=1, device_id=peer, device_id_type=MESH)

    def remote(src, dst, ssem, rsem, peer):
        return pltpu.make_async_remote_copy(
            src_ref=src, dst_ref=dst, send_sem=ssem, recv_sem=rsem,
            device_id=peer, device_id_type=MESH)

    def load_ham(b):
        part = pl.ds(b * GS, GS)
        return pltpu.make_async_copy(ham.at[part], hbuf.at[part], h_sem.at[b])

    def block_of(i):
        return jnp.where(i < 7, i + 1, jnp.where(i < 9, (8 - i) * (NG - 1), i - 1))

    def start_ham(i, c):
        load_ham(block_of(i)).start()
        return c

    load_partner = pltpu.make_async_copy(partner_in, partner, m_sem.at[0])
    live = live_in
    load_head = pltpu.make_async_copy(trial.at[pl.ds(0, HEAD)], v0a.at[pl.ds(HW, HEAD)], t_sem.at[0])
    load_trial = pltpu.make_async_copy(trial, v0.at[pl.ds(HW, S)], t_sem.at[1])
    load_partner.start()
    load_head.start()
    for i in range(3):
        load_ham(block_of(i)).start()
    load_trial.start()
    lax.fori_loop(3, NG, start_ham, 0)
    count = live[0]

    def keep(s):
        return (s < HW) | (s >= HW + S - count)

    def mask(ref, s):
        ref[s + HW] = jnp.where(keep(s), ref[s + HW].astype(F32), 0.0).astype(BF)

    def product(src, s):
        lhs = jnp.concatenate([hbuf[s, k] for k in range(K)], axis=1)
        rhs = jnp.concatenate([src[partner[k, s]] for k in range(K)], axis=0)
        return jnp.dot(lhs, rhs, preferred_element_type=F32)

    def first_step(b, src):
        for j in range(GS):
            s = b * GS + j
            value = (product(src, s) - CENTER * src[s + HW].astype(F32)) * (1.0 / HALF_WIDTH)
            v1[s + HW] = jnp.where(keep(s), value, 0.0).astype(BF)

    def second_step(g):
        for j in range(GS):
            s = g * GS + j
            value = (product(v1, s) - CENTER * v1[s + HW].astype(F32)) * (2.0 / HALF_WIDTH)
            value = value - v0[s + HW].astype(F32)
            filt[s] = jnp.where(keep(s), value, 0.0).astype(BF)

    def to_col(g, t, d):
        there = lax.rem(col + d, 4)
        return remote(filt.at[g * GS + there], recv.at[t, col], y_s.at[t, d - 1], y_r.at[t, d - 1], at_y(d))

    def from_col(t, d):
        origin = lax.rem(col + 4 - d, 4)
        return remote(filt.at[0], recv.at[t, origin], y_s.at[t, d - 1], y_r.at[t, d - 1], at_y(d))

    def hand_out(g, t):
        for d in (2, 1, 3):
            to_col(g, t, d).start()
        recv[t, col] = filt[g * GS + col]

    load_head.wait()
    lax.fori_loop(HW, HEAD, lambda s, c: (mask(v0a, s), c)[1], 0)
    load_partner.wait()

    def prologue(i, c):
        b = block_of(i)
        load_ham(b).wait()
        first_step(b, v0a)
        return c

    lax.fori_loop(0, 3, prologue, 0)
    load_trial.wait()
    lax.fori_loop(HW, S - 32, lambda s, c: (mask(v0, s), c)[1], 0)
    second_step(2)
    pl.semaphore_wait(barrier, len(peers))
    hand_out(2, 0)

    def halo(src, first, land, n):
        return (
            remote(src.at[pl.ds(first + S - HW, HW)], land.at[0], halo_s.at[n], halo_r.at[n], after),
            remote(src.at[pl.ds(first, HW)], land.at[1], halo_s.at[n + 1], halo_r.at[n + 1], before),
        )

    def place(land, dst):
        for j in range(HW):
            dst[j] = jnp.where(row > 0, land[0, j].astype(F32), 0.0).astype(BF)
            dst[j + HW + S] = jnp.where(row < 31, land[1, j].astype(F32), 0.0).astype(BF)

    halo0 = halo(trial, 0, land0, 0)
    for copy in halo0:
        copy.start()

    def main(i, c):
        b = i + 1
        load_ham(b).wait()
        first_step(b, v0)
        second_step(i)
        hand_out(i, i - 2)
        return c

    lax.fori_loop(3, 7, main, 0)

    for copy in halo0:
        copy.wait()
    place(land0, v0)

    def outer(n, c):
        b = (1 - n) * (NG - 1)
        load_ham(b).wait()
        first_step(b, v0)
        return c

    lax.fori_loop(0, 2, outer, 0)
    halo1 = halo(v1, HW, land1, 2)
    for copy in halo1:
        copy.start()

    lax.fori_loop(7, NG - 2, main, 0)

    def last(n, c):
        g = jnp.where(n == 0, NG - 2, jnp.where(n < 3, 2 - n, NG - 1))

        @pl.when(n == 2)
        def _():
            for copy in halo1:
                copy.wait()
            place(land1, v1)

        second_step(g)
        hand_out(g, NG - 4 + n)
        return c

    lax.fori_loop(0, 4, last, 0)

    gacc[...] = jnp.zeros_like(gacc)

    def gram_step(first, groups):
        for u in range(groups):
            for d in (1, 2, 3):
                from_col(first + u, d).wait_recv()
        rows = [jnp.concatenate([recv[first + u, q] for q in range(4)], axis=1) for u in range(groups)]
        x = jnp.concatenate(rows, axis=0)
        part = lax.dot_general(x, x, (((0,), (0,)), ((), ())), preferred_element_type=F32)
        gacc[...] += part.reshape(gacc.shape)

    lax.fori_loop(0, NG // 2, lambda n, c: (gram_step(2 * n, 2), c)[1], 0)

    def to_mate(z):
        part = pl.ds(z * 4, 4)
        return remote(core_out.at[part], core_in.at[part], c_s.at[z], c_r.at[z], mate)

    for z in range(4):
        for n in range(4 * z, 4 * z + 4):
            core_out[n] = gacc[2 * n + 1 - core].astype(BF)
        to_mate(z).start()

    me = pz * 4 + px
    tiles_in[me * 4 + col] = jnp.zeros((16, 128), BF)

    def send_tile(n, q):
        peer = ((n // 4) * 8 + lax.rem(n, 4) * 2 + core, q)
        return remote(tiles_out.at[n * 4 + q], tiles_in.at[me * 4 + col], p_s.at[0], p_r.at[0], peer)

    for z in range(4):
        to_mate(z).wait_recv()
        for n in range(4 * z, 4 * z + 4):
            total = gacc[2 * n + core] + core_in[n].astype(F32)
            for q in range(4):
                tiles_out[n * 4 + q] = total[:, q * 128:(q + 1) * 128].astype(BF)

        def send(m, c):
            n = z * 4 + m // 4
            q = lax.rem(m, 4)

            @pl.when((n != me) | (q != col))
            def _():
                send_tile(n, q).start()

            return c

        lax.fori_loop(0, 16, send, 0)
    total = gacc[2 * me + core] + core_in[me].astype(F32)
    for q in range(4):
        own[q] = total[:, q * 128:(q + 1) * 128]

    def finish(t, c):
        for d in (1, 2, 3):
            from_col(t, d).wait_send()
        return c

    lax.fori_loop(0, NG, finish, 0)
    for z in range(4):
        to_mate(z).wait_send()
    rest = remote(tiles_out.at[pl.ds(0, 63)], tiles_in.at[pl.ds(0, 63)], p_s.at[0], p_r.at[0], mate)
    rest.wait_recv()
    total = own[col]
    for n in range(64):
        total = total + tiles_in[n].astype(F32)
    gram[...] = total * (1.0 / (32 * S * B))
    rest.wait_send()


def store(filt, gram, filt_out, gram_out, sem):
    copies = [
        pltpu.make_async_copy(filt.at[pl.ds(n * (S // 4), S // 4)], filt_out.at[pl.ds(n * (S // 4), S // 4)], sem.at[n])
        for n in range(4)
    ]
    copies.append(pltpu.make_async_copy(gram, gram_out, sem.at[4]))
    for copy in copies:
        copy.start()
    for copy in copies:
        copy.wait()


def body(trial_block, ham_blocks, partner, live_slots):
    dma = pltpu.SemaphoreType.DMA
    hbm = pl.BlockSpec(memory_space=pltpu.HBM)
    vmem = pl.BlockSpec(memory_space=pltpu.VMEM)
    shapes = (jax.ShapeDtypeStruct((S, B, B), BF), jax.ShapeDtypeStruct((16, 128), F32))
    filtered, gram = pl.pallas_call(
        kernel,
        out_shape=shapes,
        in_specs=[hbm, hbm, hbm, pl.BlockSpec(memory_space=pltpu.SMEM)],
        out_specs=(vmem, vmem),
        scratch_shapes=[
            pltpu.SMEM((K, S), jnp.int32),
            pltpu.SMEM((1,), jnp.int32),
            pltpu.VMEM((S, K, B, B), BF),
            pltpu.VMEM((HEAD + HW, B, B), BF),
            pltpu.VMEM((S + 2 * HW, B, B), BF),
            pltpu.VMEM((S + 2 * HW, B, B), BF),
            pltpu.VMEM((2, HW, B, B), BF),
            pltpu.VMEM((2, HW, B, B), BF),
            pltpu.VMEM((NG, 4, B, B), BF),
            pltpu.VMEM((32, 16, NS), F32),
            pltpu.VMEM((16, 16, NS), BF),
            pltpu.VMEM((16, 16, NS), BF),
            pltpu.VMEM((64, 16, 128), BF),
            pltpu.VMEM((64, 16, 128), BF),
            pltpu.VMEM((4, 16, 128), F32),
            dma((2,)),
            dma((NG,)),
            dma((2,)),
            dma((4,)),
            dma((4,)),
            dma((NG, 3)),
            dma((NG, 3)),
            dma((4,)),
            dma((4,)),
            dma((1,)),
            dma((1,)),
        ],
        compiler_params=pltpu.CompilerParams(
            collective_id=0, has_side_effects=True, vmem_limit_bytes=48 << 20),
        name="filter_gram",
    )(*[pltpu.with_memory_space_constraint(a, pltpu.HBM) for a in (trial_block.reshape(S, B, B), ham_blocks, partner.T)], live_slots)
    filtered, gram = pl.pallas_call(
        store,
        out_shape=shapes,
        in_specs=[vmem, vmem],
        out_specs=(hbm, hbm),
        scratch_shapes=[dma((5,))],
        name="store",
    )(*[pltpu.with_memory_space_constraint(a, pltpu.VMEM) for a in (filtered, gram)])
    return filtered.reshape(S * B, B), gram


def solution(mesh):
    return jax.shard_map(
        body,
        mesh=mesh,
        in_specs=(P("rows", "cols"), P("rows", None, None, None), P("rows", None), P("rows")),
        out_specs=(P("rows", "cols"), P("rows", "cols")),
        check_vma=False,
    )
```

```python
import functools

import jax
import jax.numpy as jnp
from jax import lax
from jax.experimental import pallas as pl
from jax.experimental.pallas import tpu as pltpu
from jax.sharding import PartitionSpec as P

MESH = pl.DeviceIdType.MESH
HW = 4
B = 128
S = 72
K = 9
GS = 4
NG = S // GS
MID = 9
HEAD = 20
NS = 512
CENTER = 0.5
HALF_WIDTH = 1.5
BF = jnp.bfloat16
F32 = jnp.float32


def kernel(trial, ham, partner_in, live_in, filt, gram,
           partner, live, hbuf, v0a, v0, v1, land0, land1, recv, gacc,
           core_out, core_in, tiles_out, tiles_in, own,
           m_sem, h_sem, t_sem, halo_s, halo_r, y_s, y_r, c_s, c_r, p_s, p_r, relay):
    row = lax.axis_index("rows")
    col = lax.axis_index("cols")
    core = lax.rem(row, 2)
    px = lax.rem(row // 2, 4)
    pz = row // 8
    after = (lax.rem(row + 1, 32), col)
    before = (lax.rem(row + 31, 32), col)
    mate = (row + 1 - 2 * core, col)

    def at_y(d):
        return (row, lax.rem(col + d, 4))

    def at_x(d):
        return (pz * 8 + lax.rem(px + d, 4) * 2 + core, col)

    def at_z(d):
        return (lax.rem(pz + d, 4) * 8 + px * 2 + core, col)

    peers = [after, before, mate] + [f(d) for f in (at_y, at_x, at_z) for d in (1, 2, 3)]

    def remote(src, dst, ssem, rsem, peer):
        return pltpu.make_async_remote_copy(
            src_ref=src, dst_ref=dst, send_sem=ssem, recv_sem=rsem,
            device_id=peer, device_id_type=MESH)

    def load_ham(b):
        part = pl.ds(b * GS, GS)
        return pltpu.make_async_copy(ham.at[part], hbuf.at[part], h_sem.at[b])

    def block_of(i):
        return jnp.where(i < MID, i + 1, jnp.where(i < MID + 2, (MID + 1 - i) * (NG - 1), i - 1))

    def start_ham(i, c):
        load_ham(block_of(i)).start()
        return c

    load_partner = pltpu.make_async_copy(partner_in, partner, m_sem.at[0])
    live = live_in
    load_head = pltpu.make_async_copy(trial.at[pl.ds(0, HEAD)], v0a.at[pl.ds(HW, HEAD)], t_sem.at[0])
    load_trial = pltpu.make_async_copy(trial, v0.at[pl.ds(HW, S)], t_sem.at[1])
    load_head.start()
    load_ham(block_of(0)).start()
    load_partner.start()
    for i in (1, 2):
        load_ham(block_of(i)).start()
    load_trial.start()
    barrier = pltpu.get_barrier_semaphore()
    for peer in peers:
        pl.semaphore_signal(barrier, inc=1, device_id=peer, device_id_type=MESH)
    lax.fori_loop(3, NG, start_ham, 0)
    count = live[0]

    def keep(s):
        return (s < HW) | (s >= HW + S - count)

    def mask(ref, s):
        ref[s + HW] = jnp.where(keep(s), ref[s + HW], jnp.zeros((B, B), BF))

    def product(src, s):
        lhs = jnp.concatenate([hbuf[s, k] for k in range(K)], axis=1)
        rhs = jnp.concatenate([src[partner[k, s]] for k in range(K)], axis=0)
        return jnp.dot(lhs, rhs, preferred_element_type=F32)

    def first_step(b, src):
        for j in range(GS):
            s = b * GS + j
            value = (product(src, s) - CENTER * src[s + HW].astype(F32)) * (1.0 / HALF_WIDTH)
            v1[s + HW] = jnp.where(keep(s), value, 0.0).astype(BF)

    def second_step(g, src):
        for j in range(GS):
            s = g * GS + j
            value = (product(v1, s) - CENTER * v1[s + HW].astype(F32)) * (2.0 / HALF_WIDTH)
            value = value - src[s + HW].astype(F32)
            filt[s] = jnp.where(keep(s), value, 0.0).astype(BF)

    def to_col(g, t, d):
        there = lax.rem(col + d, 4)
        return remote(filt.at[g * GS + there], recv.at[t, col], y_s.at[t, d - 1], y_r.at[t, d - 1], at_y(d))

    def from_col(t, d):
        origin = lax.rem(col + 4 - d, 4)
        return remote(filt.at[0], recv.at[t, origin], y_s.at[t, d - 1], y_r.at[t, d - 1], at_y(d))

    def hand_out(g, t):
        for d in (2, 1, 3):
            to_col(g, t, d).start()
        recv[t, col] = filt[g * GS + col]

    load_head.wait()
    lax.fori_loop(HW, HEAD, lambda s, c: (mask(v0a, s), c)[1], 0)
    load_partner.wait()

    def prologue(i, c):
        b = block_of(i)
        load_ham(b).wait()
        first_step(b, v0a)
        return c

    lax.fori_loop(0, 3, prologue, 0)
    second_step(2, v0a)
    pl.semaphore_wait(barrier, len(peers))
    hand_out(2, 0)

    for d in (1, 2, 3):
        pl.semaphore_signal(relay, inc=1, device_id=at_x(d), device_id_type=MESH)

    def halo(src, first, land, n):
        return (
            remote(src.at[pl.ds(first + S - HW, HW)], land.at[0], halo_s.at[n], halo_r.at[n], after),
            remote(src.at[pl.ds(first, HW)], land.at[1], halo_s.at[n + 1], halo_r.at[n + 1], before),
        )

    def place(land, dst):
        for j in range(HW):
            dst[j] = jnp.where(row > 0, land[0, j].astype(F32), 0.0).astype(BF)
            dst[j + HW + S] = jnp.where(row < 31, land[1, j].astype(F32), 0.0).astype(BF)

    halo0 = halo(trial, 0, land0, 0)
    for copy in halo0:
        copy.start()
    load_trial.wait()
    lax.fori_loop(HW, S - 32, lambda s, c: (mask(v0, s), c)[1], 0)

    def main(i, c):
        b = i + 1
        load_ham(b).wait()
        first_step(b, v0)
        second_step(i, v0)
        hand_out(i, i - 2)
        return c

    lax.fori_loop(3, MID, main, 0)

    for copy in halo0:
        copy.wait()
    place(land0, v0)

    def outer(n, c):
        b = (1 - n) * (NG - 1)
        load_ham(b).wait()
        first_step(b, v0)
        return c

    lax.fori_loop(0, 2, outer, 0)
    halo1 = halo(v1, HW, land1, 2)
    for copy in halo1:
        copy.start()

    lax.fori_loop(MID, NG - 2, main, 0)

    pl.semaphore_wait(relay, 3)

    def last(n, c):
        g = jnp.where(n == 0, NG - 2, jnp.where(n < 3, 2 - n, NG - 1))

        @pl.when(n == 2)
        def _():
            for copy in halo1:
                copy.wait()
            place(land1, v1)

        second_step(g, v0)
        hand_out(g, NG - 4 + n)
        return c

    lax.fori_loop(0, 4, last, 0)

    gacc[...] = jnp.zeros_like(gacc)

    def gram_step(first, groups):
        for u in range(groups):
            for d in (1, 2, 3):
                from_col(first + u, d).wait_recv()
        rows = [jnp.concatenate([recv[first + u, q] for q in range(4)], axis=1) for u in range(groups)]
        x = jnp.concatenate(rows, axis=0)
        part = lax.dot_general(x, x, (((0,), (0,)), ((), ())), preferred_element_type=F32)
        gacc[...] += part.reshape(gacc.shape)

    lax.fori_loop(0, NG // 2, lambda n, c: (gram_step(2 * n, 2), c)[1], 0)

    def to_mate(z):
        part = pl.ds(z * 4, 4)
        return remote(core_out.at[part], core_in.at[part], c_s.at[z], c_r.at[z], mate)

    for z in range(4):
        for n in range(4 * z, 4 * z + 4):
            core_out[n] = gacc[2 * n + 1 - core].astype(BF)
        to_mate(z).start()

    me = pz * 4 + px
    tiles_in[me * 4 + col] = jnp.zeros((16, 128), BF)

    def send_tile(n, q):
        peer = ((n // 4) * 8 + lax.rem(n, 4) * 2 + core, q)
        return remote(tiles_out.at[n * 4 + q], tiles_in.at[me * 4 + col], p_s.at[0], p_r.at[0], peer)

    for z in range(4):
        to_mate(z).wait_recv()
        for n in range(4 * z, 4 * z + 4):
            total = gacc[2 * n + core] + core_in[n].astype(F32)
            for q in range(4):
                tiles_out[n * 4 + q] = total[:, q * 128:(q + 1) * 128].astype(BF)

        def send(m, c):
            n = z * 4 + m // 4
            q = lax.rem(m, 4)

            @pl.when((n != me) | (q != col))
            def _():
                send_tile(n, q).start()

            return c

        lax.fori_loop(0, 16, send, 0)
    total = gacc[2 * me + core] + core_in[me].astype(F32)
    for q in range(4):
        own[q] = total[:, q * 128:(q + 1) * 128]

    def finish(t, c):
        for d in (1, 2, 3):
            from_col(t, d).wait_send()
        return c

    lax.fori_loop(0, NG, finish, 0)
    for z in range(4):
        to_mate(z).wait_send()
    rest = remote(tiles_out.at[pl.ds(0, 63)], tiles_in.at[pl.ds(0, 63)], p_s.at[0], p_r.at[0], mate)
    rest.wait_recv()
    total = own[col]
    for n in range(64):
        total = total + tiles_in[n].astype(F32)
    gram[...] = total * (1.0 / (32 * S * B))
    rest.wait_send()


def store(filt, gram, filt_out, gram_out, sem):
    copies = [
        pltpu.make_async_copy(filt.at[pl.ds(n * (S // 4), S // 4)], filt_out.at[pl.ds(n * (S // 4), S // 4)], sem.at[n])
        for n in range(4)
    ]
    copies.append(pltpu.make_async_copy(gram, gram_out, sem.at[4]))
    for copy in copies:
        copy.start()
    for copy in copies:
        copy.wait()


def body(trial_block, ham_blocks, partner, live_slots):
    dma = pltpu.SemaphoreType.DMA
    hbm = pl.BlockSpec(memory_space=pltpu.HBM)
    vmem = pl.BlockSpec(memory_space=pltpu.VMEM)
    shapes = (jax.ShapeDtypeStruct((S, B, B), BF), jax.ShapeDtypeStruct((16, 128), F32))
    filtered, gram = pl.pallas_call(
        kernel,
        out_shape=shapes,
        in_specs=[hbm, hbm, hbm, pl.BlockSpec(memory_space=pltpu.SMEM)],
        out_specs=(vmem, vmem),
        scratch_shapes=[
            pltpu.SMEM((K, S), jnp.int32),
            pltpu.SMEM((1,), jnp.int32),
            pltpu.VMEM((S, K, B, B), BF),
            pltpu.VMEM((HEAD + HW, B, B), BF),
            pltpu.VMEM((S + 2 * HW, B, B), BF),
            pltpu.VMEM((S + 2 * HW, B, B), BF),
            pltpu.VMEM((2, HW, B, B), BF),
            pltpu.VMEM((2, HW, B, B), BF),
            pltpu.VMEM((NG, 4, B, B), BF),
            pltpu.VMEM((32, 16, NS), F32),
            pltpu.VMEM((16, 16, NS), BF),
            pltpu.VMEM((16, 16, NS), BF),
            pltpu.VMEM((64, 16, 128), BF),
            pltpu.VMEM((64, 16, 128), BF),
            pltpu.VMEM((4, 16, 128), F32),
            dma((2,)),
            dma((NG,)),
            dma((2,)),
            dma((4,)),
            dma((4,)),
            dma((NG, 3)),
            dma((NG, 3)),
            dma((4,)),
            dma((4,)),
            dma((1,)),
            dma((1,)),
            pltpu.SemaphoreType.REGULAR,
        ],
        compiler_params=pltpu.CompilerParams(
            collective_id=0, has_side_effects=True, vmem_limit_bytes=48 << 20),
        name="filter_gram",
    )(*[pltpu.with_memory_space_constraint(a, pltpu.HBM) for a in (trial_block.reshape(S, B, B), ham_blocks, partner.T)], live_slots)
    filtered, gram = pl.pallas_call(
        store,
        out_shape=shapes,
        in_specs=[vmem, vmem],
        out_specs=(hbm, hbm),
        scratch_shapes=[dma((5,))],
        name="store",
    )(*[pltpu.with_memory_space_constraint(a, pltpu.VMEM) for a in (filtered, gram)])
    return filtered.reshape(S * B, B), gram


def solution(mesh):
    return jax.shard_map(
        body,
        mesh=mesh,
        in_specs=(P("rows", "cols"), P("rows", None, None, None), P("rows", None), P("rows")),
        out_specs=(P("rows", "cols"), P("rows", "cols")),
        check_vma=False,
    )
```

```python
import functools

import jax
import jax.numpy as jnp
from jax import lax
from jax.experimental import pallas as pl
from jax.experimental.pallas import tpu as pltpu
from jax.sharding import PartitionSpec as P

MESH = pl.DeviceIdType.MESH
HW = 4
B = 128
S = 72
K = 9
GS = 4
NG = S // GS
MID = 9
HEAD = 20
NS = 512
CENTER = 0.5
HALF_WIDTH = 1.5
BF = jnp.bfloat16
F32 = jnp.float32


def kernel(trial, ham, partner_in, live_in, filt, gram,
           partner, live, hbuf, v0a, v0, v1, land0, land1, recv, gacc,
           core_out, core_in, tiles_out, tiles_in, own,
           m_sem, h_sem, t_sem, halo_s, halo_r, y_s, y_r, c_s, c_r, p_s, p_r, relay):
    row = lax.axis_index("rows")
    col = lax.axis_index("cols")
    core = lax.rem(row, 2)
    px = lax.rem(row // 2, 4)
    pz = row // 8
    after = (lax.rem(row + 1, 32), col)
    before = (lax.rem(row + 31, 32), col)
    mate = (row + 1 - 2 * core, col)

    def at_y(d):
        return (row, lax.rem(col + d, 4))

    def at_x(d):
        return (pz * 8 + lax.rem(px + d, 4) * 2 + core, col)

    def at_z(d):
        return (lax.rem(pz + d, 4) * 8 + px * 2 + core, col)

    peers = [after, before, mate] + [f(d) for f in (at_y, at_x, at_z) for d in (1, 2, 3)]

    def remote(src, dst, ssem, rsem, peer):
        return pltpu.make_async_remote_copy(
            src_ref=src, dst_ref=dst, send_sem=ssem, recv_sem=rsem,
            device_id=peer, device_id_type=MESH)

    def load_ham(b):
        part = pl.ds(b * GS, GS)
        return pltpu.make_async_copy(ham.at[part], hbuf.at[part], h_sem.at[b])

    def block_of(i):
        return jnp.where(i < MID, i + 1, jnp.where(i < MID + 2, (MID + 1 - i) * (NG - 1), i - 1))

    def start_ham(i, c):
        load_ham(block_of(i)).start()
        return c

    load_partner = pltpu.make_async_copy(partner_in, partner, m_sem.at[0])
    live = live_in
    load_head = pltpu.make_async_copy(trial.at[pl.ds(0, HEAD)], v0a.at[pl.ds(HW, HEAD)], t_sem.at[0])
    load_trial = pltpu.make_async_copy(trial, v0.at[pl.ds(HW, S)], t_sem.at[1])
    load_head.start()
    load_ham(block_of(0)).start()
    load_partner.start()
    for i in (1, 2):
        load_ham(block_of(i)).start()
    load_trial.start()
    barrier = pltpu.get_barrier_semaphore()
    for peer in peers:
        pl.semaphore_signal(barrier, inc=1, device_id=peer, device_id_type=MESH)
    lax.fori_loop(3, NG, start_ham, 0)
    count = live[0]

    def keep(s):
        return (s < HW) | (s >= HW + S - count)

    def mask(ref, s):
        ref[s + HW] = jnp.where(keep(s), ref[s + HW], jnp.zeros((B, B), BF))

    def product(src, s):
        lhs = jnp.concatenate([hbuf[s, k] for k in range(K)], axis=1)
        rhs = jnp.concatenate([src[partner[k, s]] for k in range(K)], axis=0)
        return jnp.dot(lhs, rhs, preferred_element_type=F32)

    def first_step(b, src):
        for j in range(GS):
            s = b * GS + j
            value = (product(src, s) - CENTER * src[s + HW].astype(F32)) * (1.0 / HALF_WIDTH)
            v1[s + HW] = jnp.where(keep(s), value, 0.0).astype(BF)

    def second_step(g, src):
        for j in range(GS):
            s = g * GS + j
            value = (product(v1, s) - CENTER * v1[s + HW].astype(F32)) * (2.0 / HALF_WIDTH)
            value = value - src[s + HW].astype(F32)
            filt[s] = jnp.where(keep(s), value, 0.0).astype(BF)

    def to_col(g, t, d):
        there = lax.rem(col + d, 4)
        return remote(filt.at[g * GS + there], recv.at[t, col], y_s.at[t, d - 1], y_r.at[t, d - 1], at_y(d))

    def from_col(t, d):
        origin = lax.rem(col + 4 - d, 4)
        return remote(filt.at[0], recv.at[t, origin], y_s.at[t, d - 1], y_r.at[t, d - 1], at_y(d))

    def hand_out(g, t):
        for d in (2, 1, 3):
            to_col(g, t, d).start()
        recv[t, col] = filt[g * GS + col]

    load_head.wait()
    lax.fori_loop(HW, HEAD, lambda s, c: (mask(v0a, s), c)[1], 0)
    load_partner.wait()

    def prologue(i, c):
        b = block_of(i)
        load_ham(b).wait()
        first_step(b, v0a)
        return c

    lax.fori_loop(0, 3, prologue, 0)
    second_step(2, v0a)
    pl.semaphore_wait(barrier, len(peers))
    hand_out(2, 0)

    for d in (1, 2, 3):
        pl.semaphore_signal(relay, inc=1, device_id=at_x(d), device_id_type=MESH)

    def halo(src, first, land, n):
        return (
            remote(src.at[pl.ds(first + S - HW, HW)], land.at[0], halo_s.at[n], halo_r.at[n], after),
            remote(src.at[pl.ds(first, HW)], land.at[1], halo_s.at[n + 1], halo_r.at[n + 1], before),
        )

    def place(land, dst):
        for j in range(HW):
            dst[j] = jnp.where(row > 0, land[0, j].astype(F32), 0.0).astype(BF)
            dst[j + HW + S] = jnp.where(row < 31, land[1, j].astype(F32), 0.0).astype(BF)

    halo0 = halo(trial, 0, land0, 0)
    for copy in halo0:
        copy.start()
    load_trial.wait()
    lax.fori_loop(HW, S - 32, lambda s, c: (mask(v0, s), c)[1], 0)

    def main(i, c):
        b = i + 1
        load_ham(b).wait()
        first_step(b, v0)
        second_step(i, v0)
        hand_out(i, i - 2)
        return c

    lax.fori_loop(3, MID, main, 0)

    for copy in halo0:
        copy.wait()
    place(land0, v0)

    def outer(n, c):
        b = (1 - n) * (NG - 1)
        load_ham(b).wait()
        first_step(b, v0)
        return c

    lax.fori_loop(0, 2, outer, 0)
    halo1 = halo(v1, HW, land1, 2)
    for copy in halo1:
        copy.start()

    lax.fori_loop(MID, NG - 2, main, 0)

    pl.semaphore_wait(relay, 3)

    def last(n, c):
        g = jnp.where(n == 0, NG - 2, jnp.where(n < 3, 2 - n, NG - 1))

        @pl.when(n == 2)
        def _():
            for copy in halo1:
                copy.wait()
            place(land1, v1)

        second_step(g, v0)
        hand_out(g, NG - 4 + n)
        return c

    lax.fori_loop(0, 4, last, 0)

    gacc[...] = jnp.zeros_like(gacc)

    def gram_step(first, groups):
        for u in range(groups):
            for d in (1, 2, 3):
                from_col(first + u, d).wait_recv()
        rows = [jnp.concatenate([recv[first + u, q] for q in range(4)], axis=1) for u in range(groups)]
        x = jnp.concatenate(rows, axis=0)
        part = lax.dot_general(x, x, (((0,), (0,)), ((), ())), preferred_element_type=F32)
        gacc[...] += part.reshape(gacc.shape)

    lax.fori_loop(0, NG // 2, lambda n, c: (gram_step(2 * n, 2), c)[1], 0)

    def to_mate(z):
        part = pl.ds(z * 4, 4)
        return remote(core_out.at[part], core_in.at[part], c_s.at[z], c_r.at[z], mate)

    for z in range(4):
        for n in range(4 * z, 4 * z + 4):
            core_out[n] = gacc[2 * n + 1 - core].astype(BF)
        to_mate(z).start()

    me = pz * 4 + px
    tiles_in[me * 4 + col] = jnp.zeros((16, 128), BF)

    def send_tile(n, q):
        peer = ((n // 4) * 8 + lax.rem(n, 4) * 2 + core, q)
        return remote(tiles_out.at[n * 4 + q], tiles_in.at[me * 4 + col], p_s.at[0], p_r.at[0], peer)

    for z in range(4):
        to_mate(z).wait_recv()
        for n in range(4 * z, 4 * z + 4):
            total = gacc[2 * n + core] + core_in[n].astype(F32)
            for q in range(4):
                tiles_out[n * 4 + q] = total[:, q * 128:(q + 1) * 128].astype(BF)

        def send(m, c):
            n = z * 4 + m // 4
            q = lax.rem(m, 4)

            @pl.when((n != me) | (q != col))
            def _():
                send_tile(n, q).start()

            return c

        lax.fori_loop(0, 16, send, 0)
    total = gacc[2 * me + core] + core_in[me].astype(F32)
    for q in range(4):
        own[q] = total[:, q * 128:(q + 1) * 128]

    def finish(t, c):
        for d in (1, 2, 3):
            from_col(t, d).wait_send()
        return c

    lax.fori_loop(0, NG, finish, 0)
    for z in range(4):
        to_mate(z).wait_send()
    rest = remote(tiles_out.at[pl.ds(0, 63)], tiles_in.at[pl.ds(0, 63)], p_s.at[0], p_r.at[0], mate)
    rest.wait_recv()
    total = own[col]
    for n in range(64):
        total = total + tiles_in[n].astype(F32)
    gram[...] = total * (1.0 / (32 * S * B))
    rest.wait_send()


def store(filt, gram, filt_out, gram_out, sem):
    copies = [
        pltpu.make_async_copy(gram, gram_out, sem.at[0]),
        pltpu.make_async_copy(filt, filt_out, sem.at[1]),
    ]
    for copy in copies:
        copy.start()
    for copy in copies:
        copy.wait()


def body(trial_block, ham_blocks, partner, live_slots):
    dma = pltpu.SemaphoreType.DMA
    hbm = pl.BlockSpec(memory_space=pltpu.HBM)
    vmem = pl.BlockSpec(memory_space=pltpu.VMEM)
    shapes = (jax.ShapeDtypeStruct((S, B, B), BF), jax.ShapeDtypeStruct((16, 128), F32))
    filtered, gram = pl.pallas_call(
        kernel,
        out_shape=shapes,
        in_specs=[hbm, hbm, hbm, pl.BlockSpec(memory_space=pltpu.SMEM)],
        out_specs=(vmem, vmem),
        scratch_shapes=[
            pltpu.SMEM((K, S), jnp.int32),
            pltpu.SMEM((1,), jnp.int32),
            pltpu.VMEM((S, K, B, B), BF),
            pltpu.VMEM((HEAD + HW, B, B), BF),
            pltpu.VMEM((S + 2 * HW, B, B), BF),
            pltpu.VMEM((S + 2 * HW, B, B), BF),
            pltpu.VMEM((2, HW, B, B), BF),
            pltpu.VMEM((2, HW, B, B), BF),
            pltpu.VMEM((NG, 4, B, B), BF),
            pltpu.VMEM((32, 16, NS), F32),
            pltpu.VMEM((16, 16, NS), BF),
            pltpu.VMEM((16, 16, NS), BF),
            pltpu.VMEM((64, 16, 128), BF),
            pltpu.VMEM((64, 16, 128), BF),
            pltpu.VMEM((4, 16, 128), F32),
            dma((2,)),
            dma((NG,)),
            dma((2,)),
            dma((4,)),
            dma((4,)),
            dma((NG, 3)),
            dma((NG, 3)),
            dma((4,)),
            dma((4,)),
            dma((1,)),
            dma((1,)),
            pltpu.SemaphoreType.REGULAR,
        ],
        compiler_params=pltpu.CompilerParams(
            collective_id=0, has_side_effects=True, vmem_limit_bytes=48 << 20),
        name="filter_gram",
    )(*[pltpu.with_memory_space_constraint(a, pltpu.HBM) for a in (trial_block.reshape(S, B, B), ham_blocks, partner.T)], live_slots)
    filtered, gram = pl.pallas_call(
        store,
        out_shape=shapes,
        in_specs=[vmem, vmem],
        out_specs=(hbm, hbm),
        scratch_shapes=[dma((2,))],
        name="store",
    )(*[pltpu.with_memory_space_constraint(a, pltpu.VMEM) for a in (filtered, gram)])
    return filtered.reshape(S * B, B), gram


def solution(mesh):
    return jax.shard_map(
        body,
        mesh=mesh,
        in_specs=(P("rows", "cols"), P("rows", None, None, None), P("rows", None), P("rows")),
        out_specs=(P("rows", "cols"), P("rows", "cols")),
        check_vma=False,
    )
```
